128 devices in a mesh: dp: 32 (over z_lo, x, y), row: 2 (over core), col: 2 (over z_hi).
Axes of the slice: x: 4, y: 4, z: 4 (z_hi: 2, z_lo: 2; z = z_hi * 2 + z_lo), core: 2. Of those that a mesh axis runs over, the one named last changes fastest.
Arguments:
- tokens: bfloat16 [16384, 896], P('dp', 'row'), may hold values from -6 to 6
- sequence_lengths: int32 [32, 2], P('dp'), may hold values from 0 to 512, as said below
- attention_gain: float32 [896], P('row'), may hold values from 0.25 to 1.75
- packed_weight: bfloat16 [896, 1152], P('row', 'col'), may hold values from -0.1875 to 0.1875
- packed_bias: float32 [1152], P('col'), may hold values from -3 to 3
- output_weight: bfloat16 [896, 896], P('col', 'row'), may hold values from -0.75 to 0.75
- feedforward_gain: float32 [896], P('row'), may hold values from 0.25 to 1.75
- gate_weight: bfloat16 [896, 4864], P('row', 'col'), may hold values from -0.1875 to 0.1875
- up_weight: bfloat16 [896, 4864], P('row', 'col'), may hold values from -0.1875 to 0.1875
- down_weight: bfloat16 [4864, 896], P('col', 'row'), may hold values from -0.3125 to 0.3125
- upstream_gradient: bfloat16 [16384, 896], P('dp', 'row'), may hold values from -6 to 6
Outputs:
- layer_output: bfloat16 [16384, 896], P('dp', 'row')
- tokens_gradient: bfloat16 [16384, 896], P('dp', 'row')
- attention_gain_gradient: float32 [896], P('row')
- packed_weight_gradient: float32 [896, 1152], P('row', 'col')
- packed_bias_gradient: float32 [1152], P('col')
- output_weight_gradient: float32 [896, 896], P('col', 'row')
- feedforward_gain_gradient: float32 [896], P('row')
- gate_weight_gradient: float32 [896, 4864], P('row', 'col')
- up_weight_gradient: float32 [896, 4864], P('row', 'col')
- down_weight_gradient: float32 [4864, 896], P('col', 'row')
The draws below stay inside these ranges and needn't reach their ends.
Inputs may be any that keep to these rules, and one draw needn't show every extreme that they name: `sequence_lengths`: row g holds the lengths of the two sequences at the start of data group g's 512 slots, the rest being padding; the first is longer than 256, the two together are at most 512, and in every draw the first sequence of some group fills all 512 slots.
All inputs are finite; a program needn't handle non-finite values.
Results may differ from the reference program's by a relative error of at most 0.025.
Values may be sent and summed in bfloat16 or wider, within the bound.
No kernel may reach another device: no remote copies, remote signals or barrier semaphores. Data moves between devices by JAX's collectives and lax.ppermute only.
A program may use at most 128 MiB of HBM per device.

```python
import jax
import jax.numpy as jnp
from jax import lax

D = 896
HEADS = 14
KV_HEADS = 2
HEAD = 64
FF = 4864
QKV = 1152
GROUP_TOKENS = 512
GROUPS = 32
TOKENS = 16384
N_COL = 2


def draw_sequence_lengths(key, part):
    key = jax.random.fold_in(key, 11)
    first_key, second_key, pick_key = jax.random.split(key, 3)
    half_width = GROUP_TOKENS // 2
    first_length = jax.random.randint(first_key, (GROUPS,), half_width + 1, GROUP_TOKENS + 1)
    chosen = jax.random.randint(pick_key, (), 0, GROUPS)
    first_length = jnp.where(jnp.arange(GROUPS) == chosen, GROUP_TOKENS, first_length)
    second_length = jax.random.randint(second_key, (GROUPS,), 0, GROUP_TOKENS - first_length + 1)
    return jnp.stack([first_length, second_length], axis=1).astype(jnp.int32)


def steps_of(rng, shape, cuts, least, largest):
    loudness = 1.0
    for axis_at, blocks in cuts:
        steps = jax.random.uniform(jax.random.fold_in(jax.random.fold_in(rng, 6), axis_at), (blocks,), jnp.float32, least / len(cuts), largest / len(cuts))
        loudness = loudness * jnp.repeat(jnp.exp(steps), shape[axis_at] // blocks).reshape((-1,) + (1,) * (len(shape) - 1 - axis_at))
    return loudness


def bell_draw(stream_key, extent, deviation, limit, cuts=(), kind=jnp.bfloat16):
    array = deviation * jax.random.normal(stream_key, extent, jnp.float32)
    if cuts:
        array = array * steps_of(stream_key, extent, cuts, -0.22, 0.18)
    return jnp.clip(array, -limit, limit).astype(kind)


def setup_inputs(seed: int = 0) -> dict:
    splits = jax.random.split(jax.random.key(seed), 12)
    return {
        "tokens": bell_draw(splits[0], (TOKENS, D), 1.0, 6.0, ((0, 32), (1, 2))),
        "sequence_lengths": draw_sequence_lengths(jax.random.fold_in(splits[11], 71), 0),
        "attention_gain": jnp.clip(1.0 + 0.15 * jax.random.normal(splits[2], (D,), jnp.float32), 0.25, 1.75),
        "packed_weight": bell_draw(splits[3], (D, QKV), D ** -0.5, 0.1875, ((0, 2), (1, 2))),
        "packed_bias": bell_draw(splits[4], (QKV,), 0.5, 3.0, ((0, 2),), jnp.float32),
        "output_weight": bell_draw(splits[5], (D, D), (D // 16) ** -0.5, 0.75, ((0, 2), (1, 2))),
        "feedforward_gain": jnp.clip(1.0 + 0.15 * jax.random.normal(splits[6], (D,), jnp.float32), 0.25, 1.75),
        "gate_weight": bell_draw(splits[7], (D, FF), D ** -0.5, 0.1875, ((0, 2), (1, 2))),
        "up_weight": bell_draw(splits[8], (D, FF), D ** -0.5, 0.1875, ((0, 2), (1, 2))),
        "down_weight": bell_draw(splits[9], (FF, D), (FF // 16) ** -0.5, 0.3125, ((0, 2), (1, 2))),
        "upstream_gradient": bell_draw(splits[10], (TOKENS, D), 1.0, 6.0, ((0, 32), (1, 2))),
    }


@jax.custom_vjp
def low(v):
    return lax.optimization_barrier(v.astype(jnp.bfloat16)).astype(jnp.float32)

@jax.custom_vjp
def low_back(v):
    return v

def low_keep(v):
    return (low(v), None)

def low_pass(kept, grad):
    return (grad,)

def back_keep(v):
    return (v, None)

def back_low(kept, grad):
    return (low(grad),)
low.defvjp(low_keep, low_pass)
low_back.defvjp(back_keep, back_low)
EPSILON = 1e-06
ROPE_BASE = 1000000.0
MASK_FILL = -1e+30
HIGHEST_PRECISION = lax.Precision.HIGHEST

def matmul(left_side, right_side):
    return jnp.dot(left_side, right_side, precision=HIGHEST_PRECISION, preferred_element_type=jnp.float32)

def rms_scale(values):
    return lax.rsqrt(lax.optimization_barrier(jnp.mean(values * values, axis=-1, keepdims=True)) + EPSILON)

def rotate_pairs(values, cosine_table, sine_table):
    half_width = values.shape[-1] // 2
    swapped = jnp.concatenate([-values[..., half_width:], values[..., :half_width]], axis=-1)
    return values * cosine_table + swapped * sine_table

def layout(lengths, token_index):
    first_length = lengths[0]
    second_end = first_length + lengths[1]
    segment = jnp.where(token_index < first_length, 0, jnp.where(token_index < second_end, 1, -1)).astype(jnp.int32)
    segment_start = jnp.where(token_index < first_length, 0, jnp.where(token_index < second_end, first_length, second_end)).astype(jnp.int32)
    return (segment, token_index - segment_start)

def group_forward(inputs, attention_gain, packed_weight, packed_bias, output_weight, feedforward_gain, gate_weight, up_weight, down_weight, segment, cosine_table, sine_table):
    row_count = inputs.shape[0]
    query_width = HEADS // N_COL * HEAD
    key_width = KV_HEADS // N_COL * HEAD
    normed_one = low(inputs * rms_scale(inputs) * attention_gain)
    packed = low_back(matmul(normed_one, packed_weight) + packed_bias)
    packed = packed.reshape(row_count, N_COL, query_width + 2 * key_width)
    queries = packed[:, :, :query_width].reshape(row_count, HEADS, HEAD)
    new_keys = packed[:, :, query_width:query_width + key_width].reshape(row_count, KV_HEADS, HEAD)
    new_values = packed[:, :, query_width + key_width:].reshape(row_count, KV_HEADS, HEAD)
    queries = low(rotate_pairs(queries, cosine_table[:, None], sine_table[:, None]))
    new_keys = low(rotate_pairs(new_keys, cosine_table[:, None], sine_table[:, None]))
    new_values = low(new_values)
    group_size = HEADS // KV_HEADS
    new_keys = jnp.repeat(new_keys, group_size, axis=1)
    new_values = jnp.repeat(new_values, group_size, axis=1)
    scores = low_back(jnp.einsum('qhd,khd->hqk', queries, new_keys, precision=HIGHEST_PRECISION) * HEAD ** (-0.5))
    token_index = jnp.arange(row_count, dtype=jnp.int32)
    allowed = (segment[:, None] == segment[None, :]) & (segment[:, None] >= 0) & (token_index[None, :] <= token_index[:, None]) | (token_index[None, :] == token_index[:, None])
    masked = jnp.where(allowed[None], scores, MASK_FILL)
    row_top = lax.optimization_barrier(jnp.max(masked, axis=-1, keepdims=True))
    exp_scores = jnp.exp(masked - row_top)
    probs_full = exp_scores / lax.optimization_barrier(jnp.sum(exp_scores, axis=-1, keepdims=True))
    attended = jnp.einsum('hqk,khd->qhd', low(probs_full), new_values, precision=HIGHEST_PRECISION).reshape(row_count, HEADS * HEAD)
    attended = low_back(low(attended))
    branch = low_back(matmul(attended, output_weight))
    middle = inputs + branch
    normed_two = low(middle * rms_scale(middle) * feedforward_gain)
    gate_part = low_back(matmul(normed_two, gate_weight))
    up_part = low_back(matmul(normed_two, up_weight))
    hidden = low(jax.nn.silu(gate_part) * up_part)
    return middle + matmul(hidden, down_weight)

def reference(tokens, sequence_lengths, attention_gain, packed_weight, packed_bias, output_weight, feedforward_gain, gate_weight, up_weight, down_weight, upstream_gradient):
    weights = tuple((item.astype(jnp.float32) for item in (attention_gain, packed_weight, packed_bias, output_weight, feedforward_gain, gate_weight, up_weight, down_weight)))
    group_count = tokens.shape[0] // GROUP_TOKENS
    inputs_all = tokens.astype(jnp.float32).reshape(group_count, GROUP_TOKENS, D)
    cotangents = upstream_gradient.astype(jnp.float32).reshape(group_count, GROUP_TOKENS, D)
    frequency = ROPE_BASE ** (-(jnp.arange(HEAD // 2).astype(jnp.float32) * 2.0 / HEAD))

    def group_step(running, group_item):
        inputs, cotangent, lengths = group_item
        segment, position = layout(lengths, jnp.arange(GROUP_TOKENS, dtype=jnp.int32))
        angles = position.astype(jnp.float32)[:, None] * frequency[None, :]
        angles = jnp.concatenate([angles, angles], axis=-1)
        cosine_table = jnp.cos(angles)
        sine_table = jnp.sin(angles)

        def forward(inputs, *params):
            return group_forward(inputs, *params, segment, cosine_table, sine_table)
        result, pullback = jax.vjp(jax.checkpoint(forward), inputs, *weights)
        gradients = pullback(cotangent)
        running = jax.tree.map(jnp.add, running, tuple(gradients[1:]))
        return (running, (result.astype(jnp.bfloat16), gradients[0].astype(jnp.bfloat16)))
    starting = tuple((jnp.zeros_like(item) for item in weights))
    totals, (outputs, input_grads) = lax.scan(group_step, starting, (inputs_all, cotangents, sequence_lengths))
    return (outputs.reshape(tokens.shape), input_grads.reshape(tokens.shape), totals[0], totals[1], totals[2], totals[3], totals[4], totals[5], totals[6], totals[7])
```

```python
import jax
import numpy as np
import jax.numpy as jnp
from jax import lax
from jax.experimental import pallas as pl
from jax.experimental.pallas import tpu as pltpu
from jax.sharding import PartitionSpec as P

D = 896
HEADS = 14
KV_HEADS = 2
HEAD = 64
DP = 32

EPSILON = 1e-06
ROPE_BASE = 1000000.0
MASK_FILL = -1e30
F32 = jnp.float32
BF16 = jnp.bfloat16

ROW_SWAP = [(0, 1), (1, 0)]


def contract_rows(left_side, right_side):
    return lax.dot_general(
        left_side, right_side, (((0,), (0,)), ((), ())), preferred_element_type=F32
    )


def contract_last(left_side, right_side):
    return lax.dot_general(
        left_side, right_side, (((1,), (1,)), ((), ())), preferred_element_type=F32
    )


def mul(left_side, right_side):
    return jnp.dot(left_side, right_side, preferred_element_type=F32)


def row_swap(values):
    return lax.ppermute(values, "row", ROW_SWAP)


def col_swap(values):
    return lax.ppermute(values, "col", ROW_SWAP)


def cube_partner(index, dim):
    z, x, y = index >> 4, (index >> 2) & 3, index & 3
    if dim == 0:
        x ^= 1
    elif dim == 1:
        y ^= 1
    elif dim == 2:
        x ^= 3
    elif dim == 3:
        y ^= 3
    else:
        z ^= 1
    return z * 16 + x * 4 + y


def cube_bits():
    index = lax.axis_index("dp")
    z, x, y = index >> 4, (index >> 2) & 3, index & 3
    return [(x ^ (x >> 1)) & 1, (y ^ (y >> 1)) & 1, x >> 1, y >> 1, z]


CUBE_PERMS = [[(i, cube_partner(i, dim)) for i in range(DP)] for dim in range(5)]


def cube_send(values, dim):
    return lax.ppermute(values, "dp", CUBE_PERMS[dim])


def after(values, *others):
    return lax.optimization_barrier((values,) + others)[0]


SMEM = pl.BlockSpec(memory_space=pltpu.SMEM)
PARAMS = pltpu.CompilerParams(vmem_limit_bytes=58 * 1024 * 1024)
SMALL_PARAMS = pltpu.CompilerParams(vmem_limit_bytes=24 * 1024 * 1024)


def whole_call(body, outs, scratch=(), cost=None, smem=1, params=SMALL_PARAMS):
    def whole(shape):
        return pl.BlockSpec(shape, lambda i, shape=shape: (0,) * len(shape))

    def call(*arrays):
        return pl.pallas_call(
            body,
            grid=(1,),
            out_shape=[jax.ShapeDtypeStruct(shape, kind) for shape, kind in outs],
            in_specs=[
                SMEM if k < smem else whole(array.shape)
                for k, array in enumerate(arrays)
            ],
            out_specs=[whole(shape) for shape, _ in outs],
            scratch_shapes=list(scratch),
            compiler_params=params,
            cost_estimate=cost,
        )(*arrays)

    return call


def fold_small(source, got, small_own, small_got, bits, dim, place):
    rows, columns = got.shape
    half = rows // 2
    small_half = 512
    lead = small_half + (128 if place == 0 else 0)
    shape = (half, lead + columns)
    small_rows = slice(place * half, (place + 1) * half)

    def body(bits_ref, source_ref, got_ref, own_ref, other_ref, send_ref, keep_ref):
        bit = bits_ref[dim]
        for index, out_ref in ((1 - bit, send_ref), (bit, keep_ref)):
            at = pl.ds(pl.multiple_of(index * half, 16), half)
            out_ref[:, lead:] = (
                source_ref[at, :].astype(F32) + got_ref[at, :].astype(F32)
            ).astype(BF16)
            lanes = pl.ds(pl.multiple_of(index * small_half, small_half), small_half)
            out_ref[:, :small_half] = (
                own_ref[small_rows, lanes] + other_ref[small_rows, lanes].astype(F32)
            ).astype(BF16)
            if place == 0:
                vectors = slice(2 * small_half, 2 * small_half + 128)
                out_ref[:, small_half:lead] = (
                    own_ref[small_rows, vectors] + other_ref[small_rows, vectors].astype(F32)
                ).astype(BF16)

    return whole_call(body, [(shape, BF16)] * 2)(bits, source, got, small_own, small_got)


def add_kernel(mine, got, bits):
    def body(bits_ref, mine_ref, got_ref, out_ref):
        out_ref[...] = (mine_ref[...].astype(F32) + got_ref[...].astype(F32)).astype(BF16)

    return whole_call(body, [(mine.shape, BF16)])(bits, mine, got)[0]


def fold_columns(source, got, bits, dim):
    rows, columns = got.shape
    half = columns // 2

    def body(bits_ref, source_ref, got_ref, send_ref, keep_ref):
        bit = bits_ref[dim]
        for index, out_ref in ((1 - bit, send_ref), (bit, keep_ref)):
            lanes = pl.ds(pl.multiple_of(index * half, 128), half)
            out_ref[...] = (
                source_ref[:, lanes].astype(F32) + got_ref[:, lanes].astype(F32)
            ).astype(BF16)

    return whole_call(body, [((rows, half), BF16)] * 2)(bits, source, got)


def join(mine, got, bits, dim, axis):
    rows, columns = mine.shape
    shape = (2 * rows, columns) if axis == 0 else (rows, 2 * columns)

    def body(bits_ref, mine_ref, got_ref, out_ref):
        bit = bits_ref[dim]
        for index, ref in ((bit, mine_ref), (1 - bit, got_ref)):
            if axis == 0:
                out_ref[pl.ds(pl.multiple_of(index * rows, 16), rows), :] = ref[...]
            else:
                out_ref[:, pl.ds(pl.multiple_of(index * columns, 128), columns)] = ref[...]

    return whole_call(body, [(shape, BF16)])(bits, mine, got)[0]


FIRST_DIM = (1, 3, 2, 0)


class CubePart:
    def __init__(self, send, keep, place, bits):
        self.place = place
        self.dims = [(FIRST_DIM[place] + step) % 5 for step in range(5)]
        self.bits = bits
        self.send, self.source = send, keep
        self.step = 0
        self.got = None

    def start(self):
        self.got = cube_send(self.send, self.dims[(0, 1, 2, 3, 4, 2, 1, 0)[self.step]])

    def finish(self, small, *ready):
        self.got = after(self.got, *ready)
        if self.step == 0:
            self.send, self.source = fold_small(
                self.source, self.got, *small, self.bits, self.dims[1], self.place
            )
        elif self.step == 1:
            self.send, self.source = fold_columns(self.source, self.got, self.bits, self.dims[2])
        elif self.step < 5:
            self.source = add_kernel(self.source, self.got, self.bits)
            self.send = self.source
        else:
            level = 7 - self.step
            self.send = join(self.send, self.got, self.bits, self.dims[level], level - 1)
        self.step += 1


def step_all(parts, small, *ready):
    sends = tuple(part.send for part in parts)
    for part in parts:
        part.start()
    for part in parts:
        part.finish(small, *sends, *ready)
    return tuple(part.send for part in parts)


def table_constants():
    frequency = ROPE_BASE ** (-(np.arange(HEAD // 2) * 2.0 / HEAD))
    angles = np.arange(520)[:, None] * np.tile(frequency, 4)[None, :]
    return np.cos(angles).astype(np.float32), np.sin(angles).astype(np.float32)


def tables(lengths_ref, cos_ref, sin_ref, row_count):
    first = lengths_ref[0, 0]
    end = first + lengths_ref[0, 1]
    shape = (row_count, 2 * HEAD)
    index = lax.broadcasted_iota(jnp.int32, shape, 0)

    def at_start(ref):
        zero = ref[0:1, :]
        one = ref[pl.ds(first, 1), :]
        two = ref[pl.ds(end, 1), :]
        return jnp.where(index < first, zero, jnp.where(index < end, one, two))

    cos_start, sin_start = at_start(cos_ref), at_start(sin_ref)
    cos_all, sin_all = cos_ref[:row_count, :], sin_ref[:row_count, :]
    cosine = cos_all * cos_start + sin_all * sin_start
    sine = sin_all * cos_start - cos_all * sin_start
    return cosine, jnp.where(low_lanes(shape), -sine, sine)


def allowed_block(core_ref, lengths_ref, own_rows, row_count):
    first_length, second_length, core = lengths_ref[0, 0], lengths_ref[0, 1], core_ref[0]
    shape = (own_rows, row_count)
    query = core * own_rows + lax.broadcasted_iota(jnp.int32, shape, 0)
    key = lax.broadcasted_iota(jnp.int32, shape, 1)
    second_end = first_length + second_length

    def segment(index):
        return jnp.where(index < first_length, 0, jnp.where(index < second_end, 1, -1))

    query_segment = segment(query)
    same = (query_segment == segment(key)) & (query_segment >= 0) & (key <= query)
    return same | (key == query)


def low_lanes(shape):
    return (lax.broadcasted_iota(jnp.int32, shape, 1) % HEAD) < HEAD // 2


def attention_forward(scalars, lengths, tokens, tokens_other, weight, weight_other, gain, gain_other, bias, cosine, sine):
    width, row_count = tokens.shape
    own_rows = row_count // 2
    heads = HEADS // KV_HEADS
    query_width = heads * HEAD

    def body(
        scalars_ref, lengths_ref, x0_ref, x1_ref, w0_ref, w1_ref, g0_ref, g1_ref, bias_ref, cos_ref, sin_ref,
        o_ref, q_ref, kv_ref, n0_ref, n1_ref, r_ref, xo0_ref, xo1_ref,
        n0_all, n1_all, r_all, qk_all,
    ):
        own = pl.ds(pl.multiple_of(scalars_ref[0] * own_rows, own_rows), own_rows)
        xo0_ref[...] = x0_ref[:, own].astype(F32).T
        xo1_ref[...] = x1_ref[:, own].astype(F32).T
        x0 = x0_ref[...].astype(F32).T
        x1 = x1_ref[...].astype(F32).T
        squares = jnp.sum(x0 * x0, axis=1, keepdims=True) + jnp.sum(x1 * x1, axis=1, keepdims=True)
        scale = lax.rsqrt(squares / D + EPSILON)
        n0_all[...] = (x0 * scale * g0_ref[...]).astype(BF16)
        n1_all[...] = (x1 * scale * g1_ref[...]).astype(BF16)
        r_all[...] = scale
        n0_ref[...] = n0_all[own, :]
        n1_ref[...] = n1_all[own, :]
        r_ref[...] = r_all[own, :]
        packed = mul(n0_all[...], w0_ref[...]) + mul(n1_all[...], w1_ref[...]) + bias_ref[...]
        both = packed[:, : query_width + HEAD]
        full_width = query_width + HEAD
        cosine, sine = tables(lengths_ref, cos_ref, sin_ref, row_count)
        cos_all = jnp.concatenate([cosine] * (full_width // 128), axis=1)
        sin_all = jnp.concatenate([sine] * (full_width // 128), axis=1)
        swapped = jnp.where(
            low_lanes(both.shape),
            pltpu.roll(both, full_width - HEAD // 2, 1),
            pltpu.roll(both, HEAD // 2, 1),
        )
        rotated = both * cos_all + swapped * sin_all
        qk_all[...] = rotated.astype(BF16)
        key = rotated[:, query_width:].astype(BF16)
        value = packed[:, full_width:].astype(BF16)
        kv_ref[:, :HEAD] = key
        kv_ref[:, HEAD:] = value
        query = qk_all[own, :]
        q_ref[...] = query[:, :query_width]
        allowed = allowed_block(scalars_ref, lengths_ref, own_rows, row_count)
        for head in range(heads):
            lanes = slice(head * HEAD, (head + 1) * HEAD)
            scores = contract_last(query[:, lanes], key) * HEAD ** (-0.5)
            scores = jnp.where(allowed, scores, MASK_FILL)
            exp_scores = jnp.exp(scores - jnp.max(scores, axis=1, keepdims=True))
            probs = exp_scores / jnp.sum(exp_scores, axis=1, keepdims=True)
            o_ref[:, lanes] = mul(probs.astype(BF16), value).astype(BF16)

    outs = [
        ((own_rows, query_width), BF16),
        ((own_rows, query_width), BF16),
        ((row_count, 2 * HEAD), BF16),
        ((own_rows, width), BF16),
        ((own_rows, width), BF16),
        ((own_rows, 1), F32),
        ((own_rows, width), F32),
        ((own_rows, width), F32),
    ]
    scratch = [
        pltpu.VMEM((row_count, width), BF16),
        pltpu.VMEM((row_count, width), BF16),
        pltpu.VMEM((row_count, 1), F32),
        pltpu.VMEM((row_count, query_width + HEAD), BF16),
    ]
    cost = pl.CostEstimate(flops=1_100_000_000, bytes_accessed=4_000_000, transcendentals=920_000)
    return whole_call(body, outs, scratch, cost, 2, PARAMS)(
        scalars, lengths, tokens, tokens_other, weight, weight_other, gain, gain_other, bias, cosine, sine
    )


def attention_backward(
    scalars, lengths, partial, far, middle_own, middle_other, scale_two, gain, gain_other,
    upstream_own, upstream_other, attended, weight, weight_other, queries, key_value, cosine, sine,
):
    own_rows, query_width = queries.shape
    row_count = key_value.shape[0]
    width = middle_own.shape[1]
    heads = query_width // HEAD
    full_width = query_width + HEAD

    def body(
        scalars_ref, lengths_ref, p_ref, f_ref, h0_ref, h1_ref, r_ref, gain0_ref, gain1_ref, g0_ref, g1_ref,
        o_ref, w0_ref, w1_ref, q_ref, kv_ref, cos_ref, sin_ref,
        dh0_ref, dh1_ref, dgain_ref, dwo0_ref, dwo1_ref, dq_ref, keep_ref, send_ref,
        do_all, dq_all, dkv_all, cos_all, sin_all,
    ):
        core = scalars_ref[0]
        own = pl.ds(pl.multiple_of(core * own_rows, own_rows), own_rows)
        away = pl.ds(pl.multiple_of((1 - core) * own_rows, own_rows), own_rows)
        h0, h1, scale = h0_ref[...], h1_ref[...], r_ref[...]
        d0 = p_ref[0].astype(F32) + f_ref[0].astype(F32)
        d1 = p_ref[1].astype(F32) + f_ref[1].astype(F32)
        dgain_ref[0:1, :] = jnp.sum(d0 * h0 * scale, axis=0, keepdims=True)
        dgain_ref[1:2, :] = jnp.sum(d1 * h1 * scale, axis=0, keepdims=True)
        s0 = d0 * gain0_ref[...]
        s1 = d1 * gain1_ref[...]
        inner = jnp.sum(h0 * s0, axis=1, keepdims=True) + jnp.sum(h1 * s1, axis=1, keepdims=True)
        back = scale * scale * scale * inner / D
        dh0 = g0_ref[...].astype(F32) + (scale * s0 - h0 * back)
        dh1 = g1_ref[...].astype(F32) + (scale * s1 - h1 * back)
        dh0_ref[...] = dh0
        dh1_ref[...] = dh1
        low0 = dh0.astype(BF16)
        low1 = dh1.astype(BF16)
        dwo0_ref[...] = contract_rows(o_ref[...], low0)
        dwo1_ref[...] = contract_rows(o_ref[...], low1)
        do_all[...] = (
            contract_last(low0, w0_ref[...]) + contract_last(low1, w1_ref[...])
        ).astype(BF16)
        key = kv_ref[:, :HEAD]
        value = kv_ref[:, HEAD:]
        allowed = allowed_block(scalars_ref, lengths_ref, own_rows, row_count)
        key_total = jnp.zeros((row_count, HEAD), F32)
        value_total = jnp.zeros((row_count, HEAD), F32)
        dq_all[:, query_width:] = jnp.zeros((own_rows, HEAD), F32)
        for head in range(heads):
            lanes = slice(head * HEAD, (head + 1) * HEAD)
            query = q_ref[:, lanes]
            incoming = do_all[:, lanes]
            scores = contract_last(query, key) * HEAD ** (-0.5)
            scores = jnp.where(allowed, scores, MASK_FILL)
            exp_scores = jnp.exp(scores - jnp.max(scores, axis=1, keepdims=True))
            probs = exp_scores / jnp.sum(exp_scores, axis=1, keepdims=True)
            prob_gradient = contract_last(incoming, value)
            delta = jnp.sum(prob_gradient * probs, axis=1, keepdims=True)
            score_gradient = (probs * (prob_gradient - delta)).astype(BF16)
            dq_all[:, lanes] = mul(score_gradient, key) * HEAD ** (-0.5)
            key_total += contract_rows(score_gradient, query)
            value_total += contract_rows(probs.astype(BF16), incoming)
        dkv_all[:, :HEAD] = key_total * HEAD ** (-0.5)
        dkv_all[:, HEAD:] = value_total

        def rotate_back(values, cos_wide, sin_wide):
            lanes = values.shape[1]
            shifted = values * sin_wide
            return values * cos_wide + jnp.where(
                low_lanes(values.shape),
                pltpu.roll(shifted, lanes - HEAD // 2, 1),
                pltpu.roll(shifted, HEAD // 2, 1),
            )

        times = full_width // 128
        cos_all[...], sin_all[...] = tables(lengths_ref, cos_ref, sin_ref, row_count)
        cos_own = jnp.concatenate([cos_all[own, :]] * times, axis=1)
        sin_own = jnp.concatenate([sin_all[own, :]] * times, axis=1)
        dq_ref[...] = rotate_back(dq_all[...], cos_own, sin_own)[:, :query_width].astype(BF16)
        is_key = lax.broadcasted_iota(jnp.int32, (row_count, 2 * HEAD), 1) < HEAD
        cos_kv = jnp.where(is_key, cos_all[...], 1.0)
        sin_kv = jnp.where(is_key, sin_all[...], 0.0)
        dkv_all[...] = rotate_back(dkv_all[...], cos_kv, sin_kv)
        keep_ref[...] = dkv_all[own, :]
        send_ref[...] = dkv_all[away, :].astype(BF16)

    outs = [
        ((own_rows, width), F32),
        ((own_rows, width), F32),
        ((2, width), F32),
        ((query_width, width), F32),
        ((query_width, width), F32),
        ((own_rows, query_width), BF16),
        ((own_rows, 2 * HEAD), F32),
        ((own_rows, 2 * HEAD), BF16),
    ]
    scratch = [
        pltpu.VMEM((own_rows, query_width), BF16),
        pltpu.VMEM((own_rows, full_width), F32),
        pltpu.VMEM((row_count, 2 * HEAD), F32),
        pltpu.VMEM((row_count, 2 * HEAD), F32),
        pltpu.VMEM((row_count, 2 * HEAD), F32),
    ]
    cost = pl.CostEstimate(flops=4_000_000_000, bytes_accessed=8_000_000, transcendentals=920_000)
    return whole_call(body, outs, scratch, cost, 2)(
        scalars, lengths, partial, far, middle_own, middle_other, scale_two, gain, gain_other,
        upstream_own, upstream_other, attended, weight, weight_other, queries, key_value, cosine, sine,
    )


def projection_backward(
    scalars, queries_back, pair_keep, pair_got, normed_own, normed_other, inputs_own, inputs_other,
    scale, weight, weight_other, output_own, output_other, gain_two_back,
):
    own_rows, width = normed_own.shape
    query_width = queries_back.shape[1]
    packed_width = weight.shape[1]
    columns = width + packed_width

    def body(
        scalars_ref, dq_ref, keep_ref, got_ref, n0_ref, n1_ref, x0_ref, x1_ref, r_ref, w0_ref, w1_ref,
        dwo0_ref, dwo1_ref, dgain_ref, own_ref, away_ref, partial_ref, packed,
    ):
        packed[:, :query_width] = dq_ref[...]
        packed[:, query_width:] = (keep_ref[...] + got_ref[...].astype(F32)).astype(BF16)
        gradient = packed[...]
        bias = jnp.sum(gradient.astype(F32), axis=0, keepdims=True).astype(BF16)
        scale_own = r_ref[...]
        sides = (
            (n0_ref, x0_ref, w0_ref, dwo0_ref, own_ref),
            (n1_ref, x1_ref, w1_ref, dwo1_ref, away_ref),
        )
        for side, (n_ref, x_ref, w_ref, dwo_ref, out_ref) in enumerate(sides):
            kind = out_ref.dtype
            incoming = contract_last(gradient, w_ref[...])
            partial_ref[side] = incoming.astype(BF16)
            dgain = jnp.sum(incoming * x_ref[...] * scale_own, axis=0, keepdims=True)
            out_ref[:width, :width] = dwo_ref[...].astype(kind)
            out_ref[:width, width:columns] = contract_rows(n_ref[...], gradient).astype(kind)
            out_ref[:, columns:] = jnp.zeros((width, 128), kind)
            at = 0
            for vector in (dgain_ref[side : side + 1, :], bias, dgain):
                for start in range(0, vector.shape[1], 128):
                    piece = vector[:, start : start + 128]
                    out_ref[at : at + 1, columns : columns + piece.shape[1]] = piece.astype(kind)
                    at += 1

    outs = [
        ((width, columns + 128), F32),
        ((width, columns + 128), BF16),
        ((2, own_rows, width), BF16),
    ]
    scratch = [pltpu.VMEM((own_rows, packed_width), BF16)]
    cost = pl.CostEstimate(flops=1_100_000_000, bytes_accessed=9_000_000, transcendentals=0)
    return whole_call(body, outs, scratch, cost)(
        scalars, queries_back, pair_keep, pair_got, normed_own, normed_other, inputs_own, inputs_other,
        scale, weight, weight_other, output_own, output_other, gain_two_back,
    )


def small_results(pairs, width, packed_width):
    rows = pairs[0][0].shape[0]
    half = rows // 2
    leads = [640, 512, 512, 512]

    def body(*refs):
        output_ref, packed_ref, gain_two_ref, bias_ref, gain_one_ref, whole = refs[8:]
        for p in range(4):
            total = refs[2 * p][...].astype(F32) + refs[2 * p + 1][...].astype(F32)
            at = slice(p * half, (p + 1) * half)
            whole[at, :512] = total[:half, :512]
            whole[at, 512:] = total[half:, :512]
            if p == 0:
                row = 0
                for out_ref in (gain_two_ref, bias_ref, gain_one_ref):
                    for start in range(0, out_ref.shape[1], 128):
                        stop = min(start + 128, out_ref.shape[1])
                        out_ref[:, start:stop] = total[row : row + 1, 512 : 512 + stop - start]
                        row += 1
        output_ref[...] = whole[:, :width]
        packed_ref[...] = whole[:, width:]

    arrays = [array for pair in pairs for array in pair[:2]]
    shapes = [(width, width), (width, packed_width), (1, width), (1, packed_width), (1, width)]
    return pl.pallas_call(
        body,
        grid=(1,),
        in_specs=[pl.BlockSpec((rows, leads[k // 2]), lambda i: (0, 0)) for k in range(8)],
        out_specs=[pl.BlockSpec(shape, lambda i: (0, 0)) for shape in shapes],
        out_shape=[jax.ShapeDtypeStruct(shape, F32) for shape in shapes],
        scratch_shapes=[pltpu.VMEM((width, width + packed_width), F32)],
        compiler_params=SMALL_PARAMS,
    )(*arrays)


def hidden_back(scalars, upstream, upstream_other, down, down_other):
    width, row_count = upstream.shape
    own_rows = row_count // 2
    unit_count = down.shape[1]

    def body(core_ref, gt0_ref, gt1_ref, w0_ref, w1_ref, du_ref, g0_ref, g1_ref, t0_ref, t1_ref):
        own = pl.ds(pl.multiple_of(core_ref[0] * own_rows, own_rows), own_rows)
        for g_ref, t_ref, gt_ref in ((g0_ref, t0_ref, gt0_ref), (g1_ref, t1_ref, gt1_ref)):
            mine = gt_ref[:, own]
            t_ref[...] = mine
            g_ref[...] = mine.astype(F32).T.astype(BF16)
        g0, g1 = g0_ref[...], g1_ref[...]
        for start in range(0, unit_count, 512):
            at = slice(start, min(start + 512, unit_count))
            du_ref[:, at] = mul(g0, w0_ref[:, at]) + mul(g1, w1_ref[:, at])

    outs = [((own_rows, unit_count), F32)]
    outs += [((own_rows, width), BF16)] * 2 + [((width, own_rows), BF16)] * 2
    cost = pl.CostEstimate(flops=1_200_000_000, bytes_accessed=9_000_000, transcendentals=0)
    return whole_call(body, outs, (), cost)(
        scalars, upstream, upstream_other, down, down_other
    )


def feedforward(
    attended, attended_far, output, output_other, output_far, output_far_other,
    inputs_own, inputs_other, gain, gain_other, turned_back_other,
    incoming, gate, gate_other, up, up_other, plan,
):
    own_rows, query_width = attended.shape
    width = inputs_own.shape[1]
    unit_count = gate.shape[1]
    tile = 512

    def body(
        o0_ref, o1_ref, wo0_ref, wo1_ref, wf0_ref, wf1_ref, x0_ref, x1_ref, gain0_ref, gain1_ref,
        gt_ref, du_hbm, wg0_hbm, wg1_hbm, wu0_hbm, wu1_hbm,
        u_hbm, dgate_hbm, dup_hbm, s0_hbm, s1_hbm, s2_hbm, s3_hbm,
        h0_ref, h1_ref, nt0_ref, r_ref, partial_ref,
        du_ref, wg0_ref, wg1_ref, wu0_ref, wu1_ref, u_ref, dgate_ref, dup_ref,
        s0_ref, s1_ref, s2_ref, s3_ref, in_sem, out_sem,
    ):
        loads = [
            pltpu.make_async_copy(source, target, in_sem.at[k])
            for k, (source, target) in enumerate(
                (
                    (wg0_hbm, wg0_ref), (wg1_hbm, wg1_ref), (wu0_hbm, wu0_ref),
                    (wu1_hbm, wu1_ref), (du_hbm, du_ref),
                )
            )
        ]
        for load in loads:
            load.start()
        near, far = o0_ref[...], o1_ref[...]
        h0 = x0_ref[...] + (mul(near, wo0_ref[...]) + mul(far, wf0_ref[...]))
        h1 = x1_ref[...] + (mul(near, wo1_ref[...]) + mul(far, wf1_ref[...]))
        squares = jnp.sum(h0 * h0, axis=1, keepdims=True) + jnp.sum(
            h1 * h1, axis=1, keepdims=True
        )
        scale = lax.rsqrt(squares / D + EPSILON)
        h0_ref[...] = h0
        h1_ref[...] = h1
        r_ref[...] = scale
        n0 = h0 * scale * gain0_ref[...]
        n1 = h1 * scale * gain1_ref[...]
        nt0_ref[...] = n0.T.astype(BF16)
        turned_other = n1.T.astype(BF16)
        n0, n1 = n0.astype(BF16), n1.astype(BF16)
        for load in loads:
            load.wait()
        for start in range(0, unit_count, tile):
            at = slice(start, min(start + tile, unit_count))
            gate_part = mul(n0, wg0_ref[:, at]) + mul(n1, wg1_ref[:, at])
            up_part = mul(n0, wu0_ref[:, at]) + mul(n1, wu1_ref[:, at])
            back = du_ref[:, at]
            sigmoid = 1.0 / (1.0 + jnp.exp(-gate_part))
            silu = gate_part * sigmoid
            u_ref[:, at] = (silu * up_part).astype(BF16)
            dup_ref[:, at] = (back * silu).astype(BF16)
            dgate_ref[:, at] = (
                back * up_part * (sigmoid * (1.0 + gate_part * (1.0 - sigmoid)))
            ).astype(BF16)
        stores = [
            pltpu.make_async_copy(source, target, out_sem.at[k])
            for k, (source, target) in enumerate(
                ((dgate_ref, dgate_hbm), (dup_ref, dup_hbm), (u_ref, u_hbm))
            )
        ]
        for store in stores:
            store.start()
        have = {0: dgate_ref, 1: dup_ref, 2: u_ref}
        blocks = ((s0_ref, s0_hbm), (s1_ref, s1_hbm), (s2_ref, s2_hbm), (s3_ref, s3_hbm))
        for k, (pieces, (block_ref, block_hbm)) in enumerate(zip(plan, blocks)):
            for at, block in piece_blocks(pieces, turned_other, gt_ref[...], have):
                block_ref[:, at] = block.astype(BF16)
            stores.append(pltpu.make_async_copy(block_ref, block_hbm, out_sem.at[3 + k]))
            stores[-1].start()
        for side, (g_ref, w_ref) in enumerate(((wg0_ref, wu0_ref), (wg1_ref, wu1_ref))):
            partial_ref[side] = (
                contract_last(dgate_ref[...], g_ref[...]) + contract_last(dup_ref[...], w_ref[...])
            ).astype(BF16)
        for store in stores:
            store.wait()

    def fixed(*shape):
        return pl.BlockSpec(shape, lambda j, shape=shape: (0,) * len(shape))

    square = fixed(query_width, width)
    block = fixed(own_rows, width)
    anywhere = pl.BlockSpec(memory_space=pl.ANY)
    wide_shape = jax.ShapeDtypeStruct((own_rows, unit_count), BF16)
    turned = jax.ShapeDtypeStruct((width, own_rows), BF16)
    totals = [sum(stop - start for _, start, stop in pieces) for pieces in plan]
    return pl.pallas_call(
        body,
        grid=(1,),
        in_specs=[
            fixed(own_rows, query_width), fixed(own_rows, query_width),
            square, square, square, square, block, block, fixed(1, width), fixed(1, width),
            fixed(width, own_rows),
        ] + [anywhere] * 5,
        out_specs=[anywhere] * 7
        + [block] * 2
        + [fixed(width, own_rows), fixed(own_rows, 1), fixed(2, own_rows, width)],
        out_shape=[wide_shape] * 3
        + [jax.ShapeDtypeStruct((width, total), BF16) for total in totals]
        + [jax.ShapeDtypeStruct((own_rows, width), F32)] * 2
        + [
            turned,
            jax.ShapeDtypeStruct((own_rows, 1), F32),
            jax.ShapeDtypeStruct((2, own_rows, width), BF16),
        ],
        scratch_shapes=[pltpu.VMEM((own_rows, unit_count), F32)]
        + [pltpu.VMEM((width, unit_count), BF16)] * 4
        + [pltpu.VMEM((own_rows, unit_count), BF16)] * 3
        + [pltpu.VMEM((width, total), BF16) for total in totals]
        + [pltpu.SemaphoreType.DMA((5,)), pltpu.SemaphoreType.DMA((7,))],
        compiler_params=PARAMS,
        cost_estimate=pl.CostEstimate(
            flops=5_000_000_000, bytes_accessed=18_000_000, transcendentals=1_300_000
        ),
    )(
        attended, attended_far, output, output_other, output_far, output_far_other,
        inputs_own, inputs_other, gain, gain_other, turned_back_other,
        incoming, gate, gate_other, up, up_other,
    )


def piece_blocks(pieces, normed_rows, upstream_rows, have):
    at = 0
    for source, start, stop in pieces:
        left = upstream_rows if source == 2 else normed_rows
        yield slice(at, at + stop - start), mul(left, have[source][:, start:stop])
        at += stop - start


def gradient_halves(bits, pieces, turned_normed, turned_upstream, sources, got, dim):
    width = turned_normed.shape[0]
    total = sum(stop - start for _, start, stop in pieces)
    used = sorted({source for source, _, _ in pieces})
    half = width // 2

    def body(bits_ref, n_ref, g_ref, got_ref, *refs):
        have = dict(zip(used, refs))
        bit = bits_ref[dim]
        for index, out_ref in ((1 - bit, refs[-2]), (bit, refs[-1])):
            rows = pl.ds(pl.multiple_of(index * half, 16), half)
            for at, block in piece_blocks(pieces, n_ref[rows, :], g_ref[rows, :], have):
                out_ref[:, at] = (block + got_ref[rows, at].astype(F32)).astype(BF16)

    cost = pl.CostEstimate(flops=2 * 256 * width * total, bytes_accessed=5_000_000, transcendentals=0)
    return whole_call(body, [((half, total), BF16)] * 2, (), cost)(
        bits, turned_normed, turned_upstream, got, *[sources[k] for k in used]
    )


def mixed_block(scalars, hidden, down, down_other, partial):
    own_rows = hidden.shape[0]
    width = down.shape[0]

    def body(scalars_ref, u_ref, d0_ref, d1_ref, p_ref, out_ref):
        for side, d_ref in enumerate((d0_ref, d1_ref)):
            lanes = slice(side * width, (side + 1) * width)
            out_ref[:own_rows, lanes] = contract_last(u_ref[...], d_ref[...]).astype(BF16)
            out_ref[own_rows:, lanes] = p_ref[side]

    cost = pl.CostEstimate(flops=1_200_000_000, bytes_accessed=6_000_000, transcendentals=0)
    return whole_call(body, [((2 * own_rows, 2 * width), BF16)], (), cost)(
        scalars, hidden, down, down_other, partial
    )[0]


def token_results(
    scalars, middle_own, middle_other, partial, far, gain, gain_other,
    inputs_own, inputs_other, scale, back_own, back_other,
):
    own_rows, width = middle_own.shape

    def body(
        scalars_ref, h0_ref, h1_ref, p_ref, f_ref, gain0_ref, gain1_ref,
        x0_ref, x1_ref, r_ref, b0_ref, b1_ref, send_ref, keep_ref,
    ):
        def total(k):
            at = slice(k // 2 * own_rows, (k // 2 + 1) * own_rows), slice(k % 2 * width, (k % 2 + 1) * width)
            return p_ref[at].astype(F32) + f_ref[at].astype(F32)

        scale_own = r_ref[...]
        s0 = total(2) * gain0_ref[...]
        s1 = total(3) * gain1_ref[...]
        x0, x1 = x0_ref[...], x1_ref[...]
        inner = jnp.sum(x0 * s0, axis=1, keepdims=True) + jnp.sum(x1 * s1, axis=1, keepdims=True)
        shrink = scale_own * scale_own * scale_own * inner / D
        sides = ((keep_ref, h0_ref, b0_ref, x0, s0), (send_ref, h1_ref, b1_ref, x1, s1))
        for side, (out_ref, h_ref, b_ref, x, s) in enumerate(sides):
            out_ref[0] = (h_ref[...] + total(side)).astype(BF16)
            out_ref[1] = (b_ref[...] + (scale_own * s - x * shrink)).astype(BF16)

    cost = pl.CostEstimate(flops=5_000_000, bytes_accessed=6_000_000, transcendentals=0)
    return whole_call(body, [((2, own_rows, width), BF16)] * 2, (), cost)(
        scalars, middle_own, middle_other, partial, far, gain, gain_other,
        inputs_own, inputs_other, scale, back_own, back_other,
    )


def token_columns(scalars, mine, got):
    _, own_rows, width = mine.shape

    def body(scalars_ref, mine_ref, got_ref, *outs):
        core = scalars_ref[0]
        for place, ref in ((core, mine_ref), (1 - core, got_ref)):
            lanes = pl.ds(pl.multiple_of(place * own_rows, own_rows), own_rows)
            for k, out_ref in enumerate(outs):
                out_ref[:, lanes] = ref[k].astype(F32).T.astype(BF16)

    return whole_call(body, [((width, 2 * own_rows), BF16)] * 2)(scalars, mine, got)


def final_half(bits, arrays, pieces, shape, flip, results=None):
    half = arrays[0].shape[0]

    def body(bits_ref, *refs):
        sources = refs[: len(arrays)]
        outs = refs[-(3 + len(pieces) + 1) : -(len(pieces) + 1)]
        scratch = refs[-(len(pieces) + 1) : -1]
        sem = refs[-1]
        copies = []
        for k, (index, dim, begin, stop, result, column) in enumerate(pieces):
            place = 1 - bits_ref[dim] if flip else bits_ref[dim]
            scratch[k][...] = sources[index][:, begin:stop].astype(F32)
            rows = pl.ds(pl.multiple_of(place * half, 8), half)
            target = outs[result].at[rows, column : column + stop - begin]
            copies.append(pltpu.make_async_copy(scratch[k], target, sem.at[k]))
            copies[-1].start()
        for copy in copies:
            copy.wait()

    anywhere = pl.BlockSpec(memory_space=pl.ANY)
    specs = [SMEM] + [pl.BlockSpec(array.shape, lambda i: (0, 0)) for array in arrays]
    operands = [bits, *arrays]
    aliases = {}
    if results is not None:
        aliases = {len(operands) + k: k for k in range(3)}
        specs += [anywhere] * 3
        operands += list(results)
    return pl.pallas_call(
        body,
        grid=(1,),
        in_specs=specs,
        out_specs=[anywhere] * 3,
        out_shape=[jax.ShapeDtypeStruct(shape, F32)] * 3,
        scratch_shapes=[pltpu.VMEM((half, piece[3] - piece[2]), F32) for piece in pieces]
        + [pltpu.SemaphoreType.DMA((len(pieces),))],
        input_output_aliases=aliases,
        compiler_params=SMALL_PARAMS,
        cost_estimate=pl.CostEstimate(flops=0, bytes_accessed=11_000_000, transcendentals=0),
    )(*operands)


def local(
    tokens,
    sequence_lengths,
    attention_gain,
    packed_weight,
    packed_bias,
    output_weight,
    feedforward_gain,
    gate_weight,
    up_weight,
    down_weight,
    upstream_gradient,
):
    row_count, width = tokens.shape
    core = lax.axis_index("row")
    bits = jnp.stack(cube_bits()).astype(jnp.int32)
    scalars = core.astype(jnp.int32).reshape(1)
    lengths = sequence_lengths

    tokens_turned = tokens.T
    upstream_turned = upstream_gradient.T
    down_turned = down_weight.T
    tokens_other = row_swap(tokens_turned)
    packed_other = row_swap(packed_weight)
    gains = jnp.stack([attention_gain, feedforward_gain])
    gains_other = row_swap(gains)
    output_far = col_swap(after(output_weight, gains_other, tokens_other, packed_other))

    bias = packed_bias[None]

    def later(weight, *others):
        return after(weight, tokens_other, packed_other, gains_other, bias, *others)

    upstream_other = row_swap(later(upstream_turned))
    output_other = row_swap(later(output_weight))
    gate_other = row_swap(later(gate_weight))
    up_other = row_swap(later(up_weight))
    down_other = row_swap(later(down_turned))
    cosine, sine = (jnp.asarray(table) for table in table_constants())
    (
        attended, queries, key_value, normed_one_own, normed_one_other, scale_one,
        inputs_own, inputs_other,
    ) = attention_forward(
        scalars, lengths, tokens_turned, tokens_other, packed_weight, packed_other,
        gains[:1], gains_other[:1], bias, cosine, sine,
    )
    attended_far = col_swap(attended)
    output_far_other = row_swap(after(output_far, attended))
    incoming, upstream_own, upstream_away, turned_back_own, turned_back_other = hidden_back(
        scalars, after(upstream_turned, attended), upstream_other, down_turned, down_other
    )
    plan = [
        [(0, 0, 1920)],
        [(0, 1920, 2432), (1, 0, 1280)],
        [(1, 1280, 2432), (2, 0, 640)],
        [(2, 640, 2432)],
    ]
    (
        hidden, gate_gradient, up_gradient, block_0, block_1, block_2, block_3,
        middle_own, middle_other, turned_two_own, scale_two, normed_two_partial,
    ) = feedforward(
        attended, attended_far, output_weight, output_other, output_far, output_far_other,
        inputs_own, inputs_other, gains[1:], gains_other[1:], turned_back_other, incoming,
        gate_weight, gate_other, up_weight, up_other, plan,
    )
    normed_two_far = col_swap(normed_two_partial)
    sources = {0: gate_gradient, 1: up_gradient, 2: hidden}
    gots = [row_swap(block) for block in (block_0, block_1, block_2, block_3)]
    parts = []
    for p, pieces in enumerate(plan):
        send, keep = gradient_halves(
            bits, pieces, turned_two_own, turned_back_own, sources, gots[p], FIRST_DIM[p]
        )
        parts.append(CubePart(send, keep, p, bits))
    ready = tuple(part.send for part in parts)

    (
        middle_back_own, middle_back_other, gain_two_back, output_back_own, output_back_other,
        query_back, pair_keep, pair_send,
    ) = attention_backward(
        scalars, lengths, normed_two_partial, after(normed_two_far, *ready), middle_own, middle_other,
        scale_two, gains[1:], gains_other[1:], upstream_own, upstream_away, attended,
        output_weight, output_other, queries, key_value, cosine, sine,
    )
    pair_got = row_swap(pair_send)
    for part in parts:
        part.start()
    first_gots = tuple(part.got for part in parts)
    small_own, small_away, normed_one_partial = projection_backward(
        scalars, query_back, pair_keep, after(pair_got, *first_gots), normed_one_own, normed_one_other,
        inputs_own, inputs_other, scale_one, packed_weight, packed_other,
        output_back_own, output_back_other, gain_two_back,
    )
    small = (small_own, row_swap(small_away))
    for part in parts:
        part.finish(small)
    tail_partial = mixed_block(
        scalars, after(hidden, *(part.send for part in parts)), down_turned, down_other,
        normed_one_partial,
    )
    step_all(parts, small, tail_partial)
    for _ in range(5):
        ready = step_all(parts, small)
    tail_far = col_swap(after(tail_partial, ready[3]))
    for part in parts:
        part.start()
    token_send, token_keep = token_results(
        scalars, middle_own, middle_other, tail_partial, after(tail_far, *ready),
        gains[:1], gains_other[:1],
        inputs_own, inputs_other, scale_one, middle_back_own, middle_back_other,
    )

    leads = [640, 512, 512, 512]
    pieces = []
    for p, part in enumerate(plan):
        at = leads[p]
        for result, start, stop in part:
            pieces.append((p, FIRST_DIM[p], at, at + stop - start, result, start))
            at += stop - start
    shape = gate_weight.shape
    mine = [part.send for part in parts]
    results = final_half(bits, mine, pieces, shape, False)
    layer_turned, tokens_turned_gradient = token_columns(
        scalars, token_keep, row_swap(after(token_send, results[0]))
    )
    gots = [after(part.got, tokens_turned_gradient) for part in parts]
    gate_weight_gradient, up_weight_gradient, down_turned_gradient = final_half(
        bits, gots, pieces, shape, True, results
    )
    pairs = list(zip(mine, gots))
    (
        output_weight_gradient, packed_weight_gradient, gain_two_sum, bias_sum, gain_one_near,
    ) = small_results(pairs, width, packed_weight.shape[1])
    gain_one_near = gain_one_near.astype(BF16)
    gain_one_sum = gain_one_near.astype(F32) + col_swap(gain_one_near).astype(F32)

    return (
        layer_turned.T,
        tokens_turned_gradient.T,
        gain_one_sum[0],
        packed_weight_gradient,
        bias_sum[0],
        output_weight_gradient,
        gain_two_sum[0],
        gate_weight_gradient,
        up_weight_gradient,
        down_turned_gradient.T,
    )


def solution(mesh):
    return jax.shard_map(
        local,
        mesh=mesh,
        in_specs=(
            P("dp", "row"),
            P("dp", None),
            P("row"),
            P("row", "col"),
            P("col"),
            P("col", "row"),
            P("row"),
            P("row", "col"),
            P("row", "col"),
            P("col", "row"),
            P("dp", "row"),
        ),
        out_specs=(
            P("dp", "row"),
            P("dp", "row"),
            P("row"),
            P("row", "col"),
            P("col"),
            P("col", "row"),
            P("row"),
            P("row", "col"),
            P("row", "col"),
            P("col", "row"),
        ),
        check_vma=False,
    )
```
